32 devices in a mesh: groups: 2 (over x), dp: 2 (over core), fsdp: 8 (over z, y).
Axes of the slice: x: 2, y: 2, z: 4, core: 2. Of those that a mesh axis runs over, the one named last changes fastest.
Arguments:
- output_gradient: bfloat16 [28672, 2880], P(('groups', 'dp', 'fsdp')), parts along dimension 0, may hold values from -6 to 6
- hidden: bfloat16 [28672, 1536], P(('groups', 'dp', 'fsdp')), parts along dimension 0, may hold values from -6 to 6
- gates: float32 [28672], P(('groups', 'dp', 'fsdp')), parts along dimension 0, may hold values from 0.1 to 1
- counts: int32 [32, 2], P(('groups', 'dp', 'fsdp')), parts along dimension 0, may hold values from 1 to 672, 896 in all within a row
- values: bfloat16 [2, 1536, 2880], P(None, None, 'fsdp'), may hold values from -0.15625 to 0.15625
- scales: bfloat16 [2, 48, 2880], P(None, None, 'fsdp'), may hold values from 0.5 to 2, as said below
- adapter_input_maps: bfloat16 [4, 1536, 64], P('groups'), parts along dimension 0, may hold values from -0.15625 to 0.15625
- adapter_output_maps: bfloat16 [4, 64, 2880], P('groups'), parts along dimension 0, may hold values from -0.75 to 0.75
Outputs:
- grad_hidden: bfloat16 [28672, 1536], P(('groups', 'dp', 'fsdp')), parts along dimension 0
- grad_a: float32 [4, 1536, 64], P('groups', 'fsdp'), parts along dimension 0
- grad_b: float32 [4, 64, 2880], P('groups', None, 'fsdp'), parts along dimension 0
The draws below stay inside these ranges and needn't reach their ends.
There are 2 independent parts, one for each index of `groups`. The reference program is written for one: setup_inputs(seed, part) draws one part's arguments, and reference() takes and returns one part's arrays. A program takes and returns all parts, laid end to end along the dimension named above; an argument that names none is the same for every part. Nothing has to cross between parts.
Inputs may be any that keep to these rules, and one draw needn't show every extreme that they name: `counts`: each row sums to 896; no entry exceeds 672. `scales`: every entry is 0.5, 1 or 2.
All inputs are finite; a program needn't handle non-finite values.
Results may differ from the reference program's by a relative error of at most 0.0051.
Values may be sent and summed in bfloat16 or wider, within the bound.
A program may use at most 128 MiB of HBM per device.

```python
import math
import jax
import jax.numpy as jnp
import numpy as np
from jax import lax

MODEL_WIDTH = 2880
HIDDEN_UNITS = 1536
EXPERTS_ACTIVE = 2
ADAPTER_RANK = 64
QBLOCK = 32
ROWS_DEV = 896
CAP = 672
ROWS = 14336
SENDERS = 16
N_DP = 2
N_FSDP = 8


def draw_scales(key, part):
    key = jax.random.fold_in(key, 11)
    powers = jax.random.randint(key, (EXPERTS_ACTIVE, HIDDEN_UNITS // QBLOCK, MODEL_WIDTH), -1, 2)
    return jnp.exp2(powers.astype(jnp.float32)).astype(jnp.bfloat16)


def with_spikes(array, rng, source, target, blocks, factor):
    owner, partner = [(jnp.arange(array.shape[dim]) // (array.shape[dim] // blocks)).reshape([-1 if axis == dim else 1 for axis in range(array.ndim)]) for dim in (source, target)]
    chosen = jax.random.permutation(rng, blocks)[partner]
    strong = (owner == chosen) | (owner == (partner + blocks // 2) % blocks)
    return jnp.where(strong, factor * array, array)


def levels(own_key, shape, shards, low, largest):
    gain = 1.0
    for dim, shards_of in shards:
        steps = jax.random.uniform(jax.random.fold_in(jax.random.fold_in(own_key, 6), dim), (shards_of,), jnp.float32, low / len(shards), largest / len(shards))
        gain = gain * jnp.repeat(jnp.exp(steps), shape[dim] // shards_of).reshape((-1,) + (1,) * (len(shape) - 1 - dim))
    return gain


def split_up(count, total, reach, skew):
    weights = [(1 << 20) // math.isqrt(rank ** skew) + 1 for rank in range(2, count + 1)]
    spare, given = total - reach - (count - 1), [1] * (count - 1)
    while spare > 0:
        free = [i for i in range(count - 1) if given[i] < reach]
        whole, budget = sum([weights[i] for i in free]), spare
        for i in free:
            more = min(reach - given[i], max(1, budget * weights[i] // whole), spare)
            given[i] = given[i] + more
            spare = spare - more
    return np.array([reach] + given)


def ragged(own_key, number_of, total, most, skew):
    if number_of == 2:
        one = jax.random.randint(own_key, (), max(1, total - most), min(most, total - 1) + 1)
        return jnp.stack([one, total - one])
    sizes = jnp.asarray(split_up(number_of, total, most, skew), jnp.int32)
    twos = (number_of - 1) // 2
    source_of, receiver = sizes[1:1 + 2 * twos:2], sizes[2:2 + 2 * twos:2]
    room = jnp.minimum(source_of - 1, most - receiver)
    passed = jax.random.randint(jax.random.fold_in(own_key, 1), (twos,), 0, 1 << 20) % (room + 1)
    sizes = sizes.at[1:1 + 2 * twos:2].set(source_of - passed).at[2:2 + 2 * twos:2].set(receiver + passed)
    return sizes[jax.random.permutation(jax.random.fold_in(own_key, 2), number_of)]


def normal_values(key, extent, deviation, most, shards=(), held_as=jnp.bfloat16):
    entries = deviation * jax.random.normal(key, extent, jnp.float32)
    if shards:
        entries = entries * levels(key, extent, shards, -0.22, 0.18)
    return jnp.clip(entries, -most, most).astype(held_as)


def bell_draw_with(rng, dims, deviation, reach, shards, heavy, held_as=jnp.bfloat16):
    drawn = deviation * jax.random.normal(rng, dims, jnp.float32)
    if shards:
        drawn = drawn * levels(rng, dims, shards, -0.22, 0.18)
    return jnp.clip(with_spikes(drawn, jax.random.fold_in(rng, 3), *heavy), -reach, reach).astype(held_as)


def setup_inputs(seed: int = 0, part: int = 0) -> dict:
    key_of = jax.random.split(jax.random.key(seed), 9)
    part_keys = jax.random.split(jax.random.fold_in(key_of[8], part), 9)
    return {
        "output_gradient": bell_draw_with(part_keys[0], (ROWS, MODEL_WIDTH), 1.0, 6.0, ((0, 16),), (0, 1, 16, 2.0)),
        "hidden": normal_values(part_keys[1], (ROWS, HIDDEN_UNITS), 1.0, 6.0, ((0, 16),)),
        "gates": jnp.clip(0.1 + 0.9 * jax.random.uniform(part_keys[2], (ROWS,), jnp.float32) ** levels(part_keys[2], (ROWS,), ((0, 16),), -0.2, 0.2), 0.1, 1.0),
        "counts": jax.vmap(lambda own: ragged(own, EXPERTS_ACTIVE, ROWS_DEV, CAP, 0))(jax.random.split(part_keys[3], SENDERS)).reshape((SENDERS, EXPERTS_ACTIVE)).astype(jnp.int32),
        "values": normal_values(key_of[4], (EXPERTS_ACTIVE, HIDDEN_UNITS, MODEL_WIDTH), HIDDEN_UNITS ** -0.5, 0.15625, ((2, 8),)),
        "scales": draw_scales(jax.random.fold_in(key_of[8], 71), part),
        "adapter_input_maps": normal_values(part_keys[6], (EXPERTS_ACTIVE, HIDDEN_UNITS, ADAPTER_RANK), HIDDEN_UNITS ** -0.5, 0.15625),
        "adapter_output_maps": normal_values(part_keys[7], (EXPERTS_ACTIVE, ADAPTER_RANK, MODEL_WIDTH), ADAPTER_RANK ** -0.5, 0.75),
    }


adapter_scale = 0.25


def to_bfloat(tensor):
    return lax.optimization_barrier(tensor.astype(jnp.bfloat16)).astype(jnp.float32)


def expert_slices(row_data, offsets, capacity):
    padding = jnp.zeros((capacity,) + row_data.shape[1:], row_data.dtype)
    padded = jnp.concatenate([row_data, padding], axis=0)
    return jnp.stack([lax.dynamic_slice_in_dim(padded, offsets[expert].astype(jnp.int32), capacity, 0) for expert in range(offsets.shape[0])])


def reference(output_gradient, hidden, gates, counts, values, scales, adapter_input_maps, adapter_output_maps):
    weights = (values.reshape(EXPERTS_ACTIVE, HIDDEN_UNITS // QBLOCK, QBLOCK, MODEL_WIDTH) * scales[:, :, None, :]).reshape(EXPERTS_ACTIVE, HIDDEN_UNITS, MODEL_WIDTH)
    weights_wide = weights.astype(jnp.float32)
    input_map_expanded = adapter_input_maps.astype(jnp.float32)
    output_map_expanded = adapter_output_maps.astype(jnp.float32)
    senders = N_DP * N_FSDP
    blocks_in = (output_gradient.reshape(senders, ROWS_DEV, MODEL_WIDTH), hidden.reshape(senders, ROWS_DEV, HIDDEN_UNITS), gates.reshape(senders, ROWS_DEV), counts)

    def one_device(running, device_block):
        out_rows, hid_rows, gate_rows, count_row = device_block
        offsets = (jnp.cumsum(count_row) - count_row).astype(jnp.int32)
        gated_rows = to_bfloat(gate_rows[:, None] * out_rows.astype(jnp.float32))
        live_mask = lax.broadcasted_iota(jnp.int32, (EXPERTS_ACTIVE, CAP), 1) < count_row[:, None]
        slot_gradients = jnp.where(live_mask[:, :, None], expert_slices(gated_rows, offsets, CAP), jnp.zeros((), jnp.float32))
        slot_hidden_units = expert_slices(hid_rows.astype(jnp.float32), offsets, CAP)
        passthrough_gradient = jnp.einsum("ecd,ehd->ech", slot_gradients, weights_wide, precision=lax.Precision.HIGHEST)
        rank_input = to_bfloat(jnp.einsum("fik,fkb->fib", slot_hidden_units, input_map_expanded, precision=lax.Precision.HIGHEST))
        rank_gradient = to_bfloat(jnp.einsum("xoy,xby->xob", slot_gradients, output_map_expanded, precision=lax.Precision.HIGHEST))
        slot_output_rows = passthrough_gradient + adapter_scale * jnp.einsum("swm,skm->swk", rank_gradient, input_map_expanded, precision=lax.Precision.HIGHEST)
        input_map_term = adapter_scale * jnp.einsum("ino,inx->iox", slot_hidden_units, rank_gradient, precision=lax.Precision.HIGHEST)
        output_map_term = adapter_scale * jnp.einsum("lzq,lzv->lqv", rank_input, slot_gradients, precision=lax.Precision.HIGHEST)
        assembled = jnp.zeros((ROWS_DEV + CAP, HIDDEN_UNITS), jnp.float32)
        for expert in range(EXPERTS_ACTIVE):
            current = lax.dynamic_slice_in_dim(assembled, offsets[expert], CAP, 0)
            assembled = lax.dynamic_update_slice_in_dim(assembled, current + slot_output_rows[expert], offsets[expert], 0)
        grad_rows = assembled[:ROWS_DEV].astype(jnp.bfloat16)
        return (running[0] + input_map_term, running[1] + output_map_term), grad_rows

    initial_sums = (jnp.zeros((EXPERTS_ACTIVE, HIDDEN_UNITS, ADAPTER_RANK), jnp.float32), jnp.zeros((EXPERTS_ACTIVE, ADAPTER_RANK, MODEL_WIDTH), jnp.float32))
    totals, grad_rows = lax.scan(one_device, initial_sums, blocks_in)
    return grad_rows.reshape(ROWS, HIDDEN_UNITS), totals[0], totals[1]
```

```python
import functools

import jax
import jax.numpy as jnp
from jax import lax
from jax.experimental import pallas as pl
from jax.experimental.pallas import tpu as pltpu
from jax.sharding import PartitionSpec as P

HIDDEN_UNITS = 1536
EXPERTS_ACTIVE = 2
CAP = 672


adapter_scale = 0.25


def expert_slices(row_data, offsets, capacity):
    padding = jnp.zeros((capacity,) + row_data.shape[1:], row_data.dtype)
    padded = jnp.concatenate([row_data, padding], axis=0)
    return jnp.stack(
        [
            lax.dynamic_slice_in_dim(padded, offsets[expert], capacity, 0)
            for expert in range(offsets.shape[0])
        ]
    )


def dequantize(block_values, block_scales):
    experts, hidden_rows, columns = block_values.shape
    blocks = block_scales.shape[1]
    shaped = block_values.reshape(experts, blocks, hidden_rows // blocks, columns)
    return (shaped * block_scales[:, :, None, :]).reshape(experts, hidden_rows, columns)


def per_device(
    output_gradient, hidden, gates, counts, values, scales, adapter_input_maps, adapter_output_maps
):
    count_row = counts[0]
    offsets = jnp.cumsum(count_row) - count_row
    gated_rows = (gates[:, None] * output_gradient.astype(jnp.float32)).astype(jnp.bfloat16)
    live_mask = lax.broadcasted_iota(jnp.int32, (EXPERTS_ACTIVE, CAP), 1) < count_row[:, None]
    slot_gradients = jnp.where(
        live_mask[:, :, None], expert_slices(gated_rows, offsets, CAP), jnp.zeros((), jnp.bfloat16)
    )
    slot_hidden_units = expert_slices(hidden, offsets, CAP)
    halves = lax.axis_size("dp")
    share_rows = HIDDEN_UNITS // halves
    share_blocks = scales.shape[1] // halves
    position = lax.axis_index("dp")
    own_values = lax.dynamic_slice_in_dim(values, position * share_rows, share_rows, 1)
    own_scales = lax.dynamic_slice_in_dim(scales, position * share_blocks, share_blocks, 1)
    full_values, full_scales = (
        lax.all_gather(own_values, "fsdp", axis=2, tiled=True),
        lax.all_gather(own_scales, "fsdp", axis=2, tiled=True),
    )
    half_weights = dequantize(full_values, full_scales)
    passthrough_gradient = jnp.einsum(
        "ecd,end->ecn",
        slot_gradients,
        lax.all_gather(half_weights, "dp", axis=1, tiled=True),
        preferred_element_type=jnp.float32,
    )
    rank_input = jnp.einsum(
        "fik,fkb->fib", slot_hidden_units, adapter_input_maps, preferred_element_type=jnp.float32
    ).astype(jnp.bfloat16)
    rank_gradient = jnp.einsum(
        "xoy,xby->xob", slot_gradients, adapter_output_maps, preferred_element_type=jnp.float32
    ).astype(jnp.bfloat16)
    slot_output_rows = passthrough_gradient + adapter_scale * jnp.einsum(
        "swm,skm->swk", rank_gradient, adapter_input_maps, preferred_element_type=jnp.float32
    )
    input_map_term = adapter_scale * jnp.einsum(
        "ino,inx->iox", slot_hidden_units, rank_gradient, preferred_element_type=jnp.float32
    )
    output_map_term = adapter_scale * jnp.einsum(
        "lzq,lzv->lqv", rank_input, slot_gradients, preferred_element_type=jnp.float32
    )
    rows_here = output_gradient.shape[0]
    assembled = jnp.zeros((rows_here + CAP, HIDDEN_UNITS), jnp.float32)
    for expert in range(EXPERTS_ACTIVE):
        current = lax.dynamic_slice_in_dim(assembled, offsets[expert], CAP, 0)
        assembled = lax.dynamic_update_slice_in_dim(
            assembled, current + slot_output_rows[expert], offsets[expert], 0
        )
    grad_hidden = assembled[:rows_here].astype(jnp.bfloat16)
    share_a, share_b = (
        lax.psum_scatter(input_map_term, "fsdp", scatter_dimension=1, tiled=True),
        lax.psum_scatter(output_map_term, "fsdp", scatter_dimension=2, tiled=True),
    )
    grad_a, grad_b = lax.psum((share_a, share_b), "dp")
    return (grad_hidden, grad_a, grad_b)


def fits(mesh, output_gradient, hidden, values):
    peers = mesh.shape["fsdp"]
    rows = output_gradient.shape[0] // (peers * mesh.shape["dp"] * mesh.shape["groups"])
    wide = lane_padded(values.shape[2] // peers)
    total = 2 * (peers + 1) * values.shape[0] * values.shape[1] * wide
    total += 2 * peers * EXPERTS_ACTIVE * CAP * wide + rows * hidden.shape[1] * 8
    return (
        mesh.shape["groups"] == 2
        and mesh.shape["dp"] == 2
        and peers % 2 == 0
        and peers > 2
        and total < 44 * 2**20
    )


def lane_padded(size):
    return -(-size // 128) * 128


def ring_kernel(
    peers, own_ref, gated_ref, low_ref, maps_ref, terms_ref, hidden_out, terms_out,
    weights, total, sums_in, sums, sums_low, sums_got, final,
    send_right, recv_right, send_left, recv_left, send_pair, recv_pair, send_core, recv_core,
    send_half, recv_half, send_sum, recv_sum, send_final, recv_final,
):
    group, core, me = lax.axis_index("groups"), lax.axis_index("dp"), lax.axis_index("fsdp")
    last = 2 * (peers - 1)
    skip = total.shape[1] - CAP

    def place(position):
        return jnp.where(position < peers // 2, 2 * position, 2 * (peers - 1 - position) + 1)

    position = jnp.where(lax.rem(me, 2) == 0, me // 2, peers - 1 - me // 2)
    right = {"fsdp": place(lax.rem(position + 1, peers))}
    left = {"fsdp": place(lax.rem(position + peers - 1, peers))}
    pair, sibling = {"groups": 1 - group}, {"dp": 1 - core}
    mesh_id = pl.DeviceIdType.MESH

    barrier = pltpu.get_barrier_semaphore()
    for offset in range(1, peers):
        pl.semaphore_signal(
            barrier, inc=1, device_id={"fsdp": lax.rem(me + offset, peers)}, device_id_type=mesh_id
        )
    pl.semaphore_signal(barrier, inc=1, device_id=pair, device_id_type=mesh_id)
    pl.semaphore_signal(barrier, inc=1, device_id=sibling, device_id_type=mesh_id)
    pl.semaphore_wait(barrier, peers + 1)

    def remote(source, target, send_sem, recv_sem, device):
        return pltpu.make_async_remote_copy(
            src_ref=source, dst_ref=target, send_sem=send_sem, recv_sem=recv_sem,
            device_id=device, device_id_type=mesh_id,
        )

    third_right, third_left, third_pair = 2 * group, 1, 2 - 2 * group
    mine, others = 3 * core, 3 - 3 * core

    def owner_right(k):
        return place(lax.rem(position + peers - (k // 2 + 1), peers))

    def owner_left(k):
        return place(lax.rem(position + k // 2 + 1, peers))

    def right_copy(source, owner, k):
        target = weights.at[owner, mine + third_right, lax.rem(k, 2)]
        return remote(target if source is None else source, target, send_right.at[k], recv_right.at[k], right)

    def left_copy(source, owner, k):
        target = weights.at[owner, mine + third_left, lax.rem(k, 2)]
        return remote(target if source is None else source, target, send_left.at[k], recv_left.at[k], left)

    def pair_copy(k, third):
        block = weights.at[owner_right(k), mine + third, lax.rem(k, 2)]
        return remote(block, block, send_pair.at[k], recv_pair.at[k], pair)

    def core_copy(kind, k, base):
        owner = owner_left(k) if kind == 1 else owner_right(k)
        third = (third_right, third_left, third_pair)[kind]
        block = weights.at[owner, base + third, lax.rem(k, 2)]
        return remote(block, block, send_core.at[kind, k], recv_core.at[kind, k], sibling)

    for k in range(2):
        right_copy(own_ref.at[mine + third_right, k], me, k).start()
        left_copy(own_ref.at[mine + third_left, k], me, k).start()
    half_copy = remote(terms_ref.at[1 - core], sums_in, send_half, recv_half, sibling)
    half_copy.start()

    def sum_copy(offset):
        return remote(
            sums_low.at[lax.rem(me + offset, peers)], sums_got.at[offset - 1],
            send_sum.at[offset - 1], recv_sum.at[offset - 1], {"fsdp": lax.rem(me + offset, peers)},
        )

    def final_copy(which):
        return remote(final.at[which], final.at[which], send_final, recv_final, sibling)

    contract = (((1,), (1,)), ((), ()))

    def prepare(part, carry):
        total[part] = adapter_scale * lax.dot_general(
            low_ref[...], maps_ref[part], contract, preferred_element_type=jnp.float32
        )
        return carry

    lax.fori_loop(0, 6, prepare, 0)

    def add_product(block, owner, expert, part):
        rows = pl.ds(pl.multiple_of(expert * skip, 32), CAP)
        total[part, rows, :] += lax.dot_general(
            gated_ref[expert, owner], block, contract, preferred_element_type=jnp.float32
        )

    def step(k, carry):
        @pl.when(k < last)
        def _():
            right_copy(None, owner_right(k), k).wait_recv()

            @pl.when(k < last - 2)
            def _():
                right_copy(None, owner_right(k), k + 2).start()

            pair_copy(k, third_right).start()
            core_copy(0, k, mine).start()
            left_copy(None, owner_left(k), k).wait_recv()

            @pl.when(k < last - 2)
            def _():
                left_copy(None, owner_left(k), k + 2).start()

            core_copy(1, k, mine).start()

        @pl.when(k < 12)
        def _():
            add_product(own_ref[k // 2, lax.rem(k, 2)], me, lax.rem(k, 2), k // 2)

        @pl.when(k == 2)
        def _():
            half_copy.wait_recv()

            def add_half(block, carry):
                sums[block] = terms_ref[core, block] + sums_in[block]
                sums_low[block] = sums[block].astype(jnp.bfloat16)
                return carry

            lax.fori_loop(0, peers, add_half, 0)
            for offset in range(1, peers):
                sum_copy(offset).start()

        @pl.when(k == last - 3)
        def _():
            summed = sums[me]
            for offset in range(1, peers):
                sum_copy(offset).wait_recv()
                summed = summed + sums_got[offset - 1].astype(jnp.float32)
            final[core] = summed
            final_copy(core).start()

        @pl.when((k >= 1) & (k < last + 1))
        def _():
            now = k - 1
            expert = lax.rem(now, 2)
            pair_copy(now, third_pair).wait_recv()
            core_copy(2, now, mine).start()
            core_copy(0, now, others).wait_recv()
            core_copy(1, now, others).wait_recv()
            first, second = owner_right(now), owner_left(now)
            for base in (mine, others):
                part = base + third_right
                add_product(weights[first, part, expert], first, expert, part)
                part = base + third_left
                add_product(weights[second, part, expert], second, expert, part)

        @pl.when(k >= 2)
        def _():
            now = k - 2
            expert = lax.rem(now, 2)
            core_copy(2, now, others).wait_recv()
            owner = owner_right(now)
            for base in (mine, others):
                part = base + third_pair
                add_product(weights[owner, part, expert], owner, expert, part)

        return carry

    lax.fori_loop(0, last + 2, step, 0)

    for part in range(6):
        width = total.shape[2]
        hidden_out[:, part * width:(part + 1) * width] = total[part].astype(jnp.bfloat16)
    final_copy(1 - core).wait_recv()
    terms_out[...] = final[...]

    def finish(k, carry):
        right_copy(None, me, k).wait_send()
        left_copy(None, me, k).wait_send()
        pair_copy(k, third_right).wait_send()
        for kind in range(3):
            core_copy(kind, k, mine).wait_send()
        return carry

    lax.fori_loop(0, last, finish, 0)
    half_copy.wait_send()
    final_copy(core).wait_send()
    for offset in range(1, peers):
        sum_copy(offset).wait_send()


def per_device_ring(
    output_gradient, hidden, gates, counts, values, scales, adapter_input_maps, adapter_output_maps
):
    peers = lax.axis_size("fsdp")
    rows, width = output_gradient.shape
    units, rank = hidden.shape[1], adapter_input_maps.shape[2]
    columns = width // peers
    wide = lane_padded(columns)
    split = counts[0, 0]
    pad = ((0, 0), (0, 0), (0, wide - columns))
    own = jnp.pad(dequantize(values, scales), pad)
    own = own.reshape(EXPERTS_ACTIVE, 6, units // 6, wide).transpose(1, 0, 2, 3)
    gated = (gates[:, None] * output_gradient.astype(jnp.float32)).astype(jnp.bfloat16)
    blocks = jnp.pad(gated.reshape(rows, peers, columns), pad).transpose(1, 0, 2)
    row_ids = lax.broadcasted_iota(jnp.int32, (rows, 1), 0)
    first = row_ids < split
    zero = jnp.zeros((), jnp.bfloat16)
    masked = jnp.stack(
        [
            jnp.where(first[None, :CAP], blocks[:, :CAP], zero),
            jnp.where(first[None, rows - CAP:], zero, blocks[:, rows - CAP:]),
        ]
    )
    maps_in = jnp.concatenate([adapter_input_maps[0], adapter_input_maps[1]], axis=1)
    maps_out = adapter_output_maps.reshape(EXPERTS_ACTIVE * rank, width)
    of_expert = first == (lax.broadcasted_iota(jnp.int32, (1, EXPERTS_ACTIVE * rank), 1) < rank)
    low_in = jnp.dot(hidden, maps_in, preferred_element_type=jnp.float32)
    low_in = jnp.where(of_expert, low_in, 0.0).astype(jnp.bfloat16)
    low_back = jnp.einsum("rd,kd->rk", gated, maps_out, preferred_element_type=jnp.float32)
    low_back = jnp.where(of_expert, low_back, 0.0).astype(jnp.bfloat16)
    term_a = jnp.einsum("rh,rk->hk", hidden, low_back, preferred_element_type=jnp.float32)
    term_b = jnp.einsum("jrd,rk->jdk", blocks, low_in, preferred_element_type=jnp.float32)
    terms = jnp.concatenate([term_a.reshape(peers, units // peers, -1), term_b], axis=1)
    tall = terms.shape[1]
    terms = terms.reshape(peers, 2, tall // 2, 2 * rank).transpose(1, 0, 2, 3)
    maps_parts = maps_in.reshape(6, units // 6, 2 * rank)
    last = 2 * (peers - 1)
    half = (tall // 2, 2 * rank)
    dma = pltpu.SemaphoreType.DMA
    vmem = pl.BlockSpec(memory_space=pltpu.VMEM)
    grad_hidden, summed = pl.pallas_call(
        functools.partial(ring_kernel, peers),
        out_shape=(
            jax.ShapeDtypeStruct((rows, units), jnp.bfloat16),
            jax.ShapeDtypeStruct((2,) + half, jnp.float32),
        ),
        in_specs=[vmem] * 5,
        out_specs=(vmem, vmem),
        scratch_shapes=[
            pltpu.VMEM((peers,) + own.shape, jnp.bfloat16),
            pltpu.VMEM((6, rows, units // 6), jnp.float32),
            pltpu.VMEM((peers,) + half, jnp.float32),
            pltpu.VMEM((peers,) + half, jnp.float32),
            pltpu.VMEM((peers,) + half, jnp.bfloat16),
            pltpu.VMEM((peers - 1,) + half, jnp.bfloat16),
            pltpu.VMEM((2,) + half, jnp.float32),
        ]
        + [dma((last,))] * 6
        + [dma((3, last))] * 2
        + [dma, dma]
        + [dma((peers - 1,))] * 2
        + [dma, dma],
        compiler_params=pltpu.CompilerParams(
            collective_id=0, has_side_effects=True, vmem_limit_bytes=58 * 2**20
        ),
        cost_estimate=pl.CostEstimate(
            flops=2 * EXPERTS_ACTIVE * CAP * width * units, bytes_accessed=20 * 2**20, transcendentals=0
        ),
    )(own, masked, low_back, maps_parts, terms)
    summed = adapter_scale * summed.reshape(tall, EXPERTS_ACTIVE, rank)
    cut = units // peers
    grad_a = summed[:cut].transpose(1, 0, 2)
    grad_b = summed[cut:cut + columns].transpose(1, 2, 0)
    return grad_hidden, grad_a, grad_b


def solution(mesh):
    placed = (
        P(("groups", "dp", "fsdp"), None),
        P(("groups", "dp", "fsdp"), None),
        P(("groups", "dp", "fsdp")),
        P(("groups", "dp", "fsdp"), None),
        P(None, None, "fsdp"),
        P(None, None, "fsdp"),
        P("groups", None, None),
        P("groups", None, None),
    )

    def whole(output_gradient, hidden, gates, counts, values, *rest):
        ring = fits(mesh, output_gradient, hidden, values)
        return jax.shard_map(
            per_device_ring if ring else per_device,
            mesh=mesh,
            in_specs=placed,
            out_specs=(
                P(("groups", "dp", "fsdp"), None),
                P("groups", "fsdp", None),
                P("groups", None, "fsdp"),
            ),
            check_vma=False,
        )(output_gradient, hidden, gates, counts, values, *rest)

    return whole
```

```python
import functools

import jax
import jax.numpy as jnp
from jax import lax
from jax.experimental import pallas as pl
from jax.experimental.pallas import tpu as pltpu
from jax.sharding import PartitionSpec as P

HIDDEN_UNITS = 1536
EXPERTS_ACTIVE = 2
CAP = 672


adapter_scale = 0.25


def expert_slices(row_data, offsets, capacity):
    padding = jnp.zeros((capacity,) + row_data.shape[1:], row_data.dtype)
    padded = jnp.concatenate([row_data, padding], axis=0)
    return jnp.stack(
        [
            lax.dynamic_slice_in_dim(padded, offsets[expert], capacity, 0)
            for expert in range(offsets.shape[0])
        ]
    )


def dequantize(block_values, block_scales):
    experts, hidden_rows, columns = block_values.shape
    blocks = block_scales.shape[1]
    shaped = block_values.reshape(experts, blocks, hidden_rows // blocks, columns)
    return (shaped * block_scales[:, :, None, :]).reshape(experts, hidden_rows, columns)


def per_device(
    output_gradient, hidden, gates, counts, values, scales, adapter_input_maps, adapter_output_maps
):
    count_row = counts[0]
    offsets = jnp.cumsum(count_row) - count_row
    gated_rows = (gates[:, None] * output_gradient.astype(jnp.float32)).astype(jnp.bfloat16)
    live_mask = lax.broadcasted_iota(jnp.int32, (EXPERTS_ACTIVE, CAP), 1) < count_row[:, None]
    slot_gradients = jnp.where(
        live_mask[:, :, None], expert_slices(gated_rows, offsets, CAP), jnp.zeros((), jnp.bfloat16)
    )
    slot_hidden_units = expert_slices(hidden, offsets, CAP)
    halves = lax.axis_size("dp")
    share_rows = HIDDEN_UNITS // halves
    share_blocks = scales.shape[1] // halves
    position = lax.axis_index("dp")
    own_values = lax.dynamic_slice_in_dim(values, position * share_rows, share_rows, 1)
    own_scales = lax.dynamic_slice_in_dim(scales, position * share_blocks, share_blocks, 1)
    full_values, full_scales = (
        lax.all_gather(own_values, "fsdp", axis=2, tiled=True),
        lax.all_gather(own_scales, "fsdp", axis=2, tiled=True),
    )
    half_weights = dequantize(full_values, full_scales)
    passthrough_gradient = jnp.einsum(
        "ecd,end->ecn",
        slot_gradients,
        lax.all_gather(half_weights, "dp", axis=1, tiled=True),
        preferred_element_type=jnp.float32,
    )
    rank_input = jnp.einsum(
        "fik,fkb->fib", slot_hidden_units, adapter_input_maps, preferred_element_type=jnp.float32
    ).astype(jnp.bfloat16)
    rank_gradient = jnp.einsum(
        "xoy,xby->xob", slot_gradients, adapter_output_maps, preferred_element_type=jnp.float32
    ).astype(jnp.bfloat16)
    slot_output_rows = passthrough_gradient + adapter_scale * jnp.einsum(
        "swm,skm->swk", rank_gradient, adapter_input_maps, preferred_element_type=jnp.float32
    )
    input_map_term = adapter_scale * jnp.einsum(
        "ino,inx->iox", slot_hidden_units, rank_gradient, preferred_element_type=jnp.float32
    )
    output_map_term = adapter_scale * jnp.einsum(
        "lzq,lzv->lqv", rank_input, slot_gradients, preferred_element_type=jnp.float32
    )
    rows_here = output_gradient.shape[0]
    assembled = jnp.zeros((rows_here + CAP, HIDDEN_UNITS), jnp.float32)
    for expert in range(EXPERTS_ACTIVE):
        current = lax.dynamic_slice_in_dim(assembled, offsets[expert], CAP, 0)
        assembled = lax.dynamic_update_slice_in_dim(
            assembled, current + slot_output_rows[expert], offsets[expert], 0
        )
    grad_hidden = assembled[:rows_here].astype(jnp.bfloat16)
    share_a, share_b = (
        lax.psum_scatter(input_map_term, "fsdp", scatter_dimension=1, tiled=True),
        lax.psum_scatter(output_map_term, "fsdp", scatter_dimension=2, tiled=True),
    )
    grad_a, grad_b = lax.psum((share_a, share_b), "dp")
    return (grad_hidden, grad_a, grad_b)


def fits(mesh, output_gradient, hidden, values):
    peers = mesh.shape["fsdp"]
    rows = output_gradient.shape[0] // (peers * mesh.shape["dp"] * mesh.shape["groups"])
    wide = lane_padded(values.shape[2] // peers)
    total = 2 * (peers + 1) * values.shape[0] * values.shape[1] * wide
    total += 2 * peers * EXPERTS_ACTIVE * CAP * wide + rows * hidden.shape[1] * 8
    return (
        mesh.shape["groups"] == 2
        and mesh.shape["dp"] == 2
        and peers % 2 == 0
        and peers > 2
        and total < 44 * 2**20
    )


def lane_padded(size):
    return -(-size // 128) * 128


def ring_kernel(
    peers, columns, gradient_hbm, hidden_hbm, gates_ref, values_ref, scales_ref, maps_ref, back_maps_ref,
    hidden_out, terms_out,
    gradient_ref, hidden_ref, own_ref, gated_ref, low_ref, low_in_ref, terms_ref,
    weights, total, sums, sums_low, sums_got, final,
    send_right, recv_right, send_left, recv_left, send_pair, recv_pair, send_core, recv_core,
    send_half, recv_half, send_sum, recv_sum, send_final, recv_final, load_sem,
):
    group, core, me = lax.axis_index("groups"), lax.axis_index("dp"), lax.axis_index("fsdp")
    last = 2 * (peers - 1)
    skip = total.shape[1] - CAP

    def place(position):
        return jnp.where(position < peers // 2, 2 * position, 2 * (peers - 1 - position) + 1)

    position = jnp.where(lax.rem(me, 2) == 0, me // 2, peers - 1 - me // 2)
    right = {"fsdp": place(lax.rem(position + 1, peers))}
    left = {"fsdp": place(lax.rem(position + peers - 1, peers))}
    pair, sibling = {"groups": 1 - group}, {"dp": 1 - core}
    mesh_id = pl.DeviceIdType.MESH

    third_right, third_left, third_pair = 2 * group, 1, 2 - 2 * group
    mine, others = 3 * core, 3 - 3 * core
    depth, wide = own_ref.shape[2:]

    def scale_piece(expert, part):
        scale = scales_ref[expert, part].astype(jnp.float32)
        scale = jnp.broadcast_to(scale[:, None, :], (scale.shape[0], depth // scale.shape[0], columns))
        piece = values_ref[expert, part].astype(jnp.float32) * scale.reshape(depth, columns)
        own_ref[part, expert, :, :columns] = piece.astype(jnp.bfloat16)
        own_ref[part, expert, :, columns:] = jnp.zeros((depth, wide - columns), jnp.bfloat16)

    def scale_sent(expert, carry):
        scale_piece(expert, mine + third_right)
        scale_piece(expert, mine + third_left)
        return carry

    load_gradient = pltpu.make_async_copy(gradient_hbm, gradient_ref, load_sem.at[0])
    load_hidden = pltpu.make_async_copy(hidden_hbm, hidden_ref, load_sem.at[1])
    load_gradient.start()
    load_hidden.start()
    lax.fori_loop(0, 2, scale_sent, 0)
    barrier = pltpu.get_barrier_semaphore()
    for offset in range(1, peers):
        pl.semaphore_signal(
            barrier, inc=1, device_id={"fsdp": lax.rem(me + offset, peers)}, device_id_type=mesh_id
        )
    pl.semaphore_signal(barrier, inc=1, device_id=pair, device_id_type=mesh_id)
    pl.semaphore_signal(barrier, inc=1, device_id=sibling, device_id_type=mesh_id)
    pl.semaphore_wait(barrier, peers + 1)

    def remote(source, target, send_sem, recv_sem, device):
        return pltpu.make_async_remote_copy(
            src_ref=source, dst_ref=target, send_sem=send_sem, recv_sem=recv_sem,
            device_id=device, device_id_type=mesh_id,
        )

    def owner_right(k):
        return place(lax.rem(position + peers - (k // 2 + 1), peers))

    def owner_left(k):
        return place(lax.rem(position + k // 2 + 1, peers))

    def right_copy(source, owner, k):
        target = weights.at[owner, mine + third_right, lax.rem(k, 2)]
        return remote(target if source is None else source, target, send_right.at[k], recv_right.at[k], right)

    def left_copy(source, owner, k):
        target = weights.at[owner, mine + third_left, lax.rem(k, 2)]
        return remote(target if source is None else source, target, send_left.at[k], recv_left.at[k], left)

    def pair_copy(k, third):
        block = weights.at[owner_right(k), mine + third, lax.rem(k, 2)]
        return remote(block, block, send_pair.at[k], recv_pair.at[k], pair)

    def core_copy(kind, k, base):
        owner = owner_left(k) if kind == 1 else owner_right(k)
        third = (third_right, third_left, third_pair)[kind]
        block = weights.at[owner, base + third, lax.rem(k, 2)]
        return remote(block, block, send_core.at[kind, k], recv_core.at[kind, k], sibling)

    for k in range(2):
        right_copy(own_ref.at[mine + third_right, k], me, k).start()
        left_copy(own_ref.at[mine + third_left, k], me, k).start()
    half_copy = remote(terms_ref.at[1 - core], sums, send_half, recv_half, sibling)

    def sum_copy(offset):
        return remote(
            sums_low.at[lax.rem(me + offset, peers)], sums_got.at[offset - 1],
            send_sum.at[offset - 1], recv_sum.at[offset - 1], {"fsdp": lax.rem(me + offset, peers)},
        )

    def final_copy(which):
        return remote(final.at[which], final.at[which], send_final, recv_final, sibling)

    contract = (((1,), (1,)), ((), ()))

    def comm(k):
        @pl.when(k < last)
        def _():
            right_copy(None, owner_right(k), k).wait_recv()

            @pl.when(k < last - 2)
            def _():
                right_copy(None, owner_right(k), k + 2).start()

            pair_copy(k, third_right).start()
            core_copy(0, k, mine).start()
            left_copy(None, owner_left(k), k).wait_recv()

            @pl.when(k < last - 2)
            def _():
                left_copy(None, owner_left(k), k + 2).start()

            core_copy(1, k, mine).start()

        @pl.when((k >= 1) & (k <= last))
        def _():
            pair_copy(k - 1, third_pair).wait_recv()
            core_copy(2, k - 1, mine).start()

    def scale_rest(k, carry):
        part = jnp.where(k == 0, mine + third_pair, others + jnp.maximum(k - 1, 0))
        scale_piece(0, part)
        scale_piece(1, part)
        return carry

    def expert_rows(expert):
        return pl.ds(pl.multiple_of(expert * skip, 32), CAP)

    def gate_block(block):
        window = slice(block * columns, (block + 1) * columns)

        def gate_rows(k, carry):
            expert, chunk = k // 3, lax.rem(k, 3)
            rows = pl.ds(pl.multiple_of((expert + chunk) * skip, 32), skip)
            target = pl.ds(pl.multiple_of(chunk * skip, 32), skip)
            gated = gradient_ref[rows, window].astype(jnp.float32) * gates_ref[expert, rows, :]
            gated_ref[expert, block, target, :columns] = gated.astype(jnp.bfloat16)
            gated_ref[expert, block, target, columns:] = jnp.zeros((skip, wide - columns), jnp.bfloat16)
            return carry

        lax.fori_loop(0, 6, gate_rows, 0)

    def low_rank(expert, carry):
        rows = expert_rows(expert)
        low = jnp.zeros(low_in_ref.shape[1:], jnp.float32)
        for part in range(6):
            low += jnp.dot(
                hidden_ref[rows, part * depth:(part + 1) * depth], maps_ref[expert, part],
                preferred_element_type=jnp.float32,
            )
        low_in_ref[expert] = low.astype(jnp.bfloat16)
        back = jnp.zeros(low_ref.shape[1:], jnp.float32)
        for block in range(peers):
            back += lax.dot_general(
                gated_ref[expert, block, :, :columns],
                back_maps_ref[expert, :, block * columns:(block + 1) * columns],
                contract, preferred_element_type=jnp.float32,
            )
        low_ref[expert] = back.astype(jnp.bfloat16)
        return carry

    def prepare(part, carry):
        total[part] = jnp.zeros(total.shape[1:], jnp.float32)
        for expert in range(EXPERTS_ACTIVE):
            total[part, expert_rows(expert), :] += adapter_scale * lax.dot_general(
                low_ref[expert], maps_ref[expert, part], contract, preferred_element_type=jnp.float32
            )
        return carry

    def outer(low, rows):
        return lax.dot_general(
            low, rows, (((0,), (0,)), ((), ())), preferred_element_type=jnp.float32
        )

    def make_terms(expert, carry):
        cut = hidden_ref.shape[1] // peers
        for block in range(peers):
            terms_ref[expert, block, :, :wide] = outer(low_in_ref[expert], gated_ref[expert, block])
            terms_ref[expert, block, :, wide:wide + cut] = outer(
                low_ref[expert], hidden_ref[expert_rows(expert), block * cut:(block + 1) * cut]
            )
            terms_ref[expert, block, :, wide + cut:] = jnp.zeros(
                (terms_ref.shape[2], terms_ref.shape[3] - wide - cut), jnp.float32
            )
        return carry

    load_gradient.wait()
    for block in range(peers // 2):
        gate_block(block)
    comm(0)
    for block in range(peers // 2, peers):
        gate_block(block)
    comm(1)
    lax.fori_loop(0, 4, scale_rest, 0)
    load_hidden.wait()
    lax.fori_loop(0, 2, low_rank, 0)
    comm(2)
    lax.fori_loop(0, 2, make_terms, 0)
    half_copy.start()
    comm(3)
    lax.fori_loop(0, 6, prepare, 0)

    def add_product(block, owner, expert, part):
        total[part, expert_rows(expert), :] += lax.dot_general(
            gated_ref[expert, owner], block, contract, preferred_element_type=jnp.float32
        )

    def step(k, carry):
        comm(k + 4)

        @pl.when(k < 12)
        def _():
            add_product(own_ref[k // 2, lax.rem(k, 2)], me, lax.rem(k, 2), k // 2)

        @pl.when(k == 1)
        def _():
            half_copy.wait_recv()

            def add_half(block, carry):
                sums[block] = terms_ref[core, block] + sums[block]
                sums_low[block] = sums[block].astype(jnp.bfloat16)
                return carry

            lax.fori_loop(0, peers, add_half, 0)
            for offset in range(1, peers):
                sum_copy(offset).start()

        @pl.when(k == last - 3)
        def _():
            summed = sums[me]
            for offset in range(1, peers):
                sum_copy(offset).wait_recv()
                summed = summed + sums_got[offset - 1].astype(jnp.float32)
            final[core] = summed
            final_copy(core).start()

        @pl.when(k < last)
        def _():
            expert = lax.rem(k, 2)
            core_copy(0, k, others).wait_recv()
            core_copy(1, k, others).wait_recv()
            first, second = owner_right(k), owner_left(k)
            for base in (mine, others):
                part = base + third_right
                add_product(weights[first, part, expert], first, expert, part)
                part = base + third_left
                add_product(weights[second, part, expert], second, expert, part)

        @pl.when(k >= 1)
        def _():
            now = k - 1
            expert = lax.rem(now, 2)
            core_copy(2, now, others).wait_recv()
            owner = owner_right(now)
            for base in (mine, others):
                part = base + third_pair
                add_product(weights[owner, part, expert], owner, expert, part)

        return carry

    lax.fori_loop(0, last + 1, step, 0)

    for part in range(6):
        width = total.shape[2]
        hidden_out[:, part * width:(part + 1) * width] = total[part].astype(jnp.bfloat16)
    final_copy(1 - core).wait_recv()
    terms_out[...] = final[...]

    def finish(k, carry):
        right_copy(None, me, k).wait_send()
        left_copy(None, me, k).wait_send()
        pair_copy(k, third_right).wait_send()
        for kind in range(3):
            core_copy(kind, k, mine).wait_send()
        return carry

    lax.fori_loop(0, last, finish, 0)
    half_copy.wait_send()
    final_copy(core).wait_send()
    for offset in range(1, peers):
        sum_copy(offset).wait_send()


def per_device_ring(
    output_gradient, hidden, gates, counts, values, scales, adapter_input_maps, adapter_output_maps
):
    peers = lax.axis_size("fsdp")
    rows, width = output_gradient.shape
    units, rank = hidden.shape[1], adapter_input_maps.shape[2]
    columns = width // peers
    wide = lane_padded(columns)
    split = counts[0, 0]
    first = lax.broadcasted_iota(jnp.int32, (1, rows, 1), 1) < split
    of_expert = first == (lax.broadcasted_iota(jnp.int32, (EXPERTS_ACTIVE, 1, 1), 0) == 0)
    expert_gates = jnp.where(of_expert, gates[None, :, None], 0.0)
    parts = (EXPERTS_ACTIVE, 6, units // 6)
    cut = units // peers
    last = 2 * (peers - 1)
    half = (rank, wide + lane_padded(cut))
    dma = pltpu.SemaphoreType.DMA
    vmem = pl.BlockSpec(memory_space=pltpu.VMEM)
    grad_hidden, summed = pl.pallas_call(
        functools.partial(ring_kernel, peers, columns),
        out_shape=(
            jax.ShapeDtypeStruct((rows, units), jnp.bfloat16),
            jax.ShapeDtypeStruct((2,) + half, jnp.float32),
        ),
        in_specs=[pl.BlockSpec(memory_space=pl.ANY)] * 2 + [vmem] * 5,
        out_specs=(vmem, vmem),
        scratch_shapes=[
            pltpu.VMEM((rows, width), jnp.bfloat16),
            pltpu.VMEM((rows, units), jnp.bfloat16),
            pltpu.VMEM((6, EXPERTS_ACTIVE, units // 6, wide), jnp.bfloat16),
            pltpu.VMEM((EXPERTS_ACTIVE, peers, CAP, wide), jnp.bfloat16),
            pltpu.VMEM((EXPERTS_ACTIVE, CAP, rank), jnp.bfloat16),
            pltpu.VMEM((EXPERTS_ACTIVE, CAP, rank), jnp.bfloat16),
            pltpu.VMEM((EXPERTS_ACTIVE, peers) + half, jnp.float32),
            pltpu.VMEM((peers, 6, EXPERTS_ACTIVE, units // 6, wide), jnp.bfloat16),
            pltpu.VMEM((6, rows, units // 6), jnp.float32),
            pltpu.VMEM((peers,) + half, jnp.float32),
            pltpu.VMEM((peers,) + half, jnp.bfloat16),
            pltpu.VMEM((peers - 1,) + half, jnp.bfloat16),
            pltpu.VMEM((2,) + half, jnp.float32),
        ]
        + [dma((last,))] * 6
        + [dma((3, last))] * 2
        + [dma, dma]
        + [dma((peers - 1,))] * 2
        + [dma, dma, dma((2,))],
        compiler_params=pltpu.CompilerParams(
            collective_id=0, has_side_effects=True, vmem_limit_bytes=58 * 2**20
        ),
        cost_estimate=pl.CostEstimate(
            flops=2 * EXPERTS_ACTIVE * CAP * width * units, bytes_accessed=20 * 2**20, transcendentals=0
        ),
    )(
        output_gradient,
        hidden,
        expert_gates,
        values.reshape(parts + (columns,)),
        scales.reshape(EXPERTS_ACTIVE, 6, -1, columns),
        adapter_input_maps.reshape(parts + (rank,)),
        adapter_output_maps,
    )
    summed = adapter_scale * summed
    grad_a = summed[:, :, wide:wide + cut].transpose(0, 2, 1)
    grad_b = summed[:, :, :columns]
    return grad_hidden, grad_a, grad_b


def solution(mesh):
    placed = (
        P(("groups", "dp", "fsdp"), None),
        P(("groups", "dp", "fsdp"), None),
        P(("groups", "dp", "fsdp")),
        P(("groups", "dp", "fsdp"), None),
        P(None, None, "fsdp"),
        P(None, None, "fsdp"),
        P("groups", None, None),
        P("groups", None, None),
    )

    def whole(output_gradient, hidden, gates, counts, values, *rest):
        ring = fits(mesh, output_gradient, hidden, values)
        return jax.shard_map(
            per_device_ring if ring else per_device,
            mesh=mesh,
            in_specs=placed,
            out_specs=(
                P(("groups", "dp", "fsdp"), None),
                P("groups", "fsdp", None),
                P("groups", None, "fsdp"),
            ),
            check_vma=False,
        )(output_gradient, hidden, gates, counts, values, *rest)

    return whole
```
